128 devices in a mesh: segment: 4 (over y_hi, core), seq: 16 (over z, x), tp: 2 (over y_lo).
Axes of the slice: x: 4, y: 4 (y_hi: 2, y_lo: 2; y = y_hi * 2 + y_lo), z: 4, core: 2. Of those that a mesh axis runs over, the one named last changes fastest.
Arguments:
- pairs: bfloat16 [4, 4096, 2, 8192], P('segment', ('seq', 'tp')), may hold values from -4 to 4
- queries: bfloat16 [4, 1536, 8192], P('segment', None, ('seq', 'tp')), may hold values from -24 to 24
- upstream: bfloat16 [4, 1536, 8192], P('segment', None, ('seq', 'tp')), may hold values from -6 to 6
Outputs:
- context: bfloat16 [4, 1536, 8192], P('segment', None, ('seq', 'tp'))
- grad_query: bfloat16 [4, 1536, 8192], P('segment', None, ('seq', 'tp'))
- grad_pairs: bfloat16 [4, 4096, 2, 8192], P('segment', ('seq', 'tp'))
The draws below stay inside these ranges and needn't reach their ends.
All inputs are finite; a program needn't handle non-finite values.
Results may differ from the reference program's by a relative error of at most 0.011.
Values may be sent and summed in bfloat16 or wider, within the bound.
A program may use at most 128 MiB of HBM per device.

```python
import jax
import jax.numpy as jnp
from jax import lax

HEAD = 128
HH = 8192
S_ENC = 4096
T_DEC = 1536
SECTIONS = 4


def draw_pairs(key, part):
    key = jax.random.fold_in(key, 3)
    shape = (SECTIONS, S_ENC, 2, HH)
    base = jnp.clip(jax.random.normal(key, shape, jnp.float32), -4.0, 4.0)
    return base.astype(jnp.bfloat16)


def draw_queries(key, part):
    key = jax.random.fold_in(key, 5)
    shape = (SECTIONS, T_DEC, HH)
    base = jnp.clip(jax.random.normal(key, shape, jnp.float32), -4.0, 4.0)
    return base.astype(jnp.bfloat16)


def levels(key, dims, shards, smallest, top_value):
    def one(dim, parts):
        heights = jax.random.uniform(jax.random.fold_in(jax.random.fold_in(key, 6), dim), (parts,), jnp.float32, smallest / len(shards), top_value / len(shards))
        return jnp.repeat(jnp.exp(heights), dims[dim] // parts).reshape((-1,) + (1,) * (len(dims) - dim - 1))

    gain = one(*shards[0])
    for cut in shards[1:]:
        gain = gain * one(*cut)
    return gain


def bell_draw(rng, shape, width, limit, pieces=(), dtype=jnp.bfloat16):
    entries = width * jax.random.normal(rng, shape, jnp.float32)
    if pieces:
        entries = entries * levels(rng, shape, pieces, -0.22, 0.18)
    return jnp.clip(entries, -limit, limit).astype(dtype)


def setup_inputs(seed: int = 0) -> dict:
    splits = jax.random.split(jax.random.key(seed), 4)
    return {
        "pairs": draw_pairs(jax.random.fold_in(splits[3], 71), 0),
        "queries": draw_queries(jax.random.fold_in(splits[3], 71), 0),
        "upstream": bell_draw(splits[2], (SECTIONS, T_DEC, HH), 1.0, 6.0, ((0, 4), (2, 32))),
    }


def one_head(inputs):
    query_head, key_head, value_head, grad_head = inputs
    factor = HEAD ** -0.5
    scores = jnp.dot(query_head, key_head.T, preferred_element_type=jnp.float32) * factor
    row_max = jnp.max(scores, axis=1, keepdims=True)
    raised = jnp.exp(scores - row_max)
    weights = raised / jnp.sum(raised, axis=1, keepdims=True)
    weights_low = weights.astype(jnp.bfloat16)
    full_context = jnp.dot(weights_low, value_head, preferred_element_type=jnp.float32)
    row_dot = jnp.sum(grad_head.astype(jnp.float32) * full_context, axis=1, keepdims=True)
    grad_weights = jnp.dot(grad_head, value_head.T, preferred_element_type=jnp.float32)
    grad_scores = (weights * (grad_weights - row_dot) * factor).astype(jnp.bfloat16)
    grad_q = jnp.dot(grad_scores, key_head, preferred_element_type=jnp.float32).astype(jnp.bfloat16)
    grad_k = jnp.dot(grad_scores.T, query_head, preferred_element_type=jnp.float32).astype(jnp.bfloat16)
    grad_v = jnp.dot(weights_low.T, grad_head, preferred_element_type=jnp.float32).astype(jnp.bfloat16)
    return full_context.astype(jnp.bfloat16), grad_q, grad_k, grad_v


def by_head(array, sections, rows, num_heads):
    return array.reshape(sections, rows, num_heads, HEAD).transpose(0, 2, 1, 3).reshape(sections * num_heads, rows, HEAD)


def from_heads(array, sections, rows, num_heads):
    return array.reshape(sections, num_heads, rows, HEAD).transpose(0, 2, 1, 3).reshape(sections, rows, num_heads * HEAD)


def reference(pairs, queries, upstream):
    sections = queries.shape[0]
    num_heads = HH // HEAD
    rolled = jnp.roll(pairs, 1, axis=0)
    query_all = by_head(queries, sections, T_DEC, num_heads)
    grad_all = by_head(upstream, sections, T_DEC, num_heads)
    key_all = by_head(rolled[:, :, 0, :], sections, S_ENC, num_heads)
    value_all = by_head(rolled[:, :, 1, :], sections, S_ENC, num_heads)
    context, grad_query, grad_keys, grad_values = lax.map(one_head, (query_all, key_all, value_all, grad_all))
    context = from_heads(context, sections, T_DEC, num_heads)
    grad_query = from_heads(grad_query, sections, T_DEC, num_heads)
    grad_keys = from_heads(grad_keys, sections, S_ENC, num_heads)
    grad_values = from_heads(grad_values, sections, S_ENC, num_heads)
    grad_pairs = jnp.roll(jnp.stack([grad_keys, grad_values], axis=2), -1, axis=0)
    return context, grad_query, grad_pairs
```

```python
import functools
import math

import jax
import jax.numpy as jnp
from jax import lax
from jax.experimental import pallas as pl
from jax.experimental.pallas import tpu as pltpu
from jax.sharding import PartitionSpec as P

MESH = pl.DeviceIdType.MESH
HEAD = 128
FACTOR = HEAD ** -0.5
LOG_SCALE = FACTOR * math.log2(math.e)
PIECES = 4
PARTS = 8
CHUNK = 512
UNROLL = 8
f32, bf16 = jnp.float32, jnp.bfloat16


def dot(a, b, ca, cb):
    return lax.dot_general(a, b, (((ca,), (cb,)), ((), ())), preferred_element_type=f32)


def split_rows():
    row = lax.broadcasted_iota(jnp.int32, (256, 256), 0)
    col = lax.broadcasted_iota(jnp.int32, (256, 256), 1)
    want = jnp.where(row < 128, 2 * row, 2 * row - 255)
    return (col == want).astype(bf16)


def kernel(
    groups, segments, tps,
    pairs, q_hbm, g_hbm, ctx_hbm, dq_hbm, out,
    kv, q_v, g_v, ctx_v, dq_v, kk, vv, kt, vt, s_scr, p_scr, acc,
    kv_send, kv_recv, g_send, g_recv, in_sem, out_sem,
):
    seg, sq, tp = lax.axis_index("segment"), lax.axis_index("seq"), lax.axis_index("tp")
    me = sq * tps + tp
    nxt, prv = lax.rem(seg + 1, segments), lax.rem(seg + segments - 1, segments)
    rows = pairs.shape[0]
    enc_len, dec_len = kk.shape[0], q_v.shape[0]
    heads = kv.shape[0]
    width = heads * HEAD
    part = rows // PIECES

    barrier = pltpu.get_barrier_semaphore()

    def greet(i, c):
        pl.semaphore_signal(barrier, inc=1, device_id=(prv, i // tps, lax.rem(i, tps)), device_id_type=MESH)
        return c

    lax.fori_loop(0, groups, greet, 0)
    pl.semaphore_wait(barrier, groups)

    def kv_copy(h, i, p):
        col = pl.multiple_of(i * width + h * HEAD, HEAD)
        piece = pl.ds(p * part, part)
        return pltpu.make_async_remote_copy(
            src_ref=pairs.at[piece, :, pl.ds(col, HEAD)], dst_ref=kv.at[h, me, piece],
            send_sem=kv_send.at[h], recv_sem=kv_recv.at[h],
            device_id=(nxt, i // tps, lax.rem(i, tps)), device_id_type=MESH)

    def g_copy(h, i, p):
        col = pl.multiple_of(me * width + h * HEAD, HEAD)
        piece = pl.ds(p * part, part)
        return pltpu.make_async_remote_copy(
            src_ref=kv.at[h, i, piece], dst_ref=out.at[piece, :, pl.ds(col, HEAD)],
            send_sem=g_send.at[h], recv_sem=g_recv.at[h],
            device_id=(prv, i // tps, lax.rem(i, tps)), device_id_type=MESH)

    for h in range(heads):
        def send(k, c):
            kv_copy(h, lax.rem(me + k, groups), k // groups).start()
            return c
        lax.fori_loop(0, groups * PIECES, send, 0)
    loads = [pltpu.make_async_copy(q_hbm, q_v, in_sem.at[0]), pltpu.make_async_copy(g_hbm, g_v, in_sem.at[1])]
    for load in loads:
        load.start()
    for load in loads:
        load.wait()

    sel = split_rows()
    sel_t = sel.T
    per = CHUNK // rows
    chunks = enc_len // CHUNK
    stores = []
    for h in range(heads):
        hs = slice(h * HEAD, (h + 1) * HEAD)
        flat = kv.at[h].reshape(groups, 2 * rows, HEAD)
        q, g = q_v.at[:, hs], g_v.at[:, hs]
        pltpu.make_async_copy(kv.at[h], kv.at[h], kv_recv.at[h]).wait()

        def split(i, c):
            for u in range(UNROLL):
                b = i * UNROLL + u
                y = dot(sel, flat[b], 1, 0).astype(bf16)
                r = pl.multiple_of(b * rows, rows)
                kk[pl.ds(r, rows), :] = y[:rows]
                vv[pl.ds(r, rows), :] = y[rows:]
                kt[:, pl.ds(r, rows)] = y[:rows].T
                vt[:, pl.ds(r, rows)] = y[rows:].T
            return c
        lax.fori_loop(0, groups // UNROLL, split, 0)

        def scores(i, m):
            o = pl.multiple_of(i * CHUNK, CHUNK)
            s = dot(kk[pl.ds(o, CHUNK), :], q[...], 1, 1)
            s_scr[pl.ds(o, CHUNK), :] = s
            return jnp.maximum(m, jnp.max(s.reshape(CHUNK // 8, 8, dec_len), axis=0))
        m = lax.fori_loop(0, chunks, scores, jnp.full((8, dec_len), -jnp.inf, f32))
        mc = jnp.max(m, axis=0, keepdims=True) * LOG_SCALE
        acc[...] = jnp.zeros_like(acc)

        def weigh(i, l):
            o = pl.multiple_of(i * CHUNK, CHUNK)
            p = jnp.exp2(s_scr[pl.ds(o, CHUNK), :] * LOG_SCALE - mc)
            pb = p.astype(bf16)
            p_scr[pl.ds(o, CHUNK), :] = pb
            acc[...] += dot(vt[:, pl.ds(o, CHUNK)], pb, 1, 0)
            return l + jnp.sum(p.reshape(CHUNK // 8, 8, dec_len), axis=0)
        l = lax.fori_loop(0, chunks, weigh, jnp.zeros((8, dec_len), f32))
        inv = 1.0 / jnp.sum(l, axis=0, keepdims=True)
        ctx = acc[...] * inv
        ctx_v[h] = ctx.T.astype(bf16)
        stores.append(pltpu.make_async_copy(ctx_v.at[h], ctx_hbm.at[:, hs], out_sem.at[0, h]))
        stores[-1].start()
        gf = g[...].astype(f32)
        row_dot = jnp.sum(gf.T * ctx, axis=0, keepdims=True)
        inv_col = jnp.broadcast_to(inv, (HEAD, dec_len)).T
        gn = (gf * inv_col).astype(bf16)
        qn = (q[...].astype(f32) * (inv_col * FACTOR)).astype(bf16)
        acc[...] = jnp.zeros_like(acc)

        def grads(i, c):
            chunk = lax.rem(i + me // per, chunks)
            o = pl.multiple_of(chunk * CHUNK, CHUNK)
            gw = dot(vv[pl.ds(o, CHUNK), :], g[...], 1, 1)
            pb = p_scr[pl.ds(o, CHUNK), :]
            ds = (pb.astype(f32) * (gw - row_dot)).astype(bf16)
            acc[...] += dot(kt[:, pl.ds(o, CHUNK)], ds, 1, 0)
            dk = dot(ds, qn, 1, 0).astype(bf16)
            dv = dot(pb, gn, 1, 0).astype(bf16)
            for u in range(per):
                a = u * rows
                x = jnp.concatenate([dk[a:a + rows], dv[a:a + rows]], axis=0)
                flat[chunk * per + u] = dot(sel_t, x, 1, 0).astype(bf16)
            for p in range(PIECES):
                for u in range(per):
                    g_copy(h, chunk * per + u, p).start()
            return c
        lax.fori_loop(0, chunks, grads, 0)
        dq_v[h] = (acc[...] * (inv * FACTOR)).T.astype(bf16)
        stores.append(pltpu.make_async_copy(dq_v.at[h], dq_hbm.at[:, hs], out_sem.at[1, h]))
        stores[-1].start()

    for store in stores:
        store.wait()
    for h in range(heads):
        for sem in (kv_send, g_send, g_recv):
            pltpu.make_async_copy(kv.at[h], kv.at[h], sem.at[h]).wait()


def place(ctx, dq, grads, ctx_out, dq_out, grads_out, ctx_v, dq_v, grads_v, load_sem, store_sem):
    part = grads.shape[0] // PARTS
    routes = [(grads.at[pl.ds(i * part, part)], grads_v.at[pl.ds(i * part, part)], grads_out.at[pl.ds(i * part, part)]) for i in range(PARTS)]
    routes += [(ctx, ctx_v, ctx_out), (dq, dq_v, dq_out)]
    loads = [pltpu.make_async_copy(src, mid, load_sem.at[i]) for i, (src, mid, _) in enumerate(routes)]
    stores = [pltpu.make_async_copy(mid, dst, store_sem.at[i]) for i, (_, mid, dst) in enumerate(routes)]
    for load in loads:
        load.start()
    for load, store in zip(loads, stores):
        load.wait()
        store.start()
    for store in stores:
        store.wait()


def shards(pairs, queries, upstream):
    groups = lax.axis_size("seq") * lax.axis_size("tp")
    _, rows, _, columns = pairs.shape
    _, dec_len, width = queries.shape
    heads = width // HEAD
    enc_len = rows * groups
    hbm = pl.BlockSpec(memory_space=pl.ANY)
    outs = [
        jax.ShapeDtypeStruct((dec_len, width), bf16),
        jax.ShapeDtypeStruct((dec_len, width), bf16),
        jax.ShapeDtypeStruct((rows, 2, columns), bf16),
    ]
    made = pl.pallas_call(
        functools.partial(kernel, groups, lax.axis_size("segment"), lax.axis_size("tp")),
        out_shape=outs,
        in_specs=[hbm] * 3,
        out_specs=[hbm] * 3,
        scratch_shapes=[
            pltpu.VMEM((heads, groups, rows, 2, HEAD), bf16),
            pltpu.VMEM((dec_len, width), bf16),
            pltpu.VMEM((dec_len, width), bf16),
            pltpu.VMEM((heads, dec_len, HEAD), bf16),
            pltpu.VMEM((heads, dec_len, HEAD), bf16),
            pltpu.VMEM((enc_len, HEAD), bf16),
            pltpu.VMEM((enc_len, HEAD), bf16),
            pltpu.VMEM((HEAD, enc_len), bf16),
            pltpu.VMEM((HEAD, enc_len), bf16),
            pltpu.VMEM((enc_len, dec_len), f32),
            pltpu.VMEM((enc_len, dec_len), bf16),
            pltpu.VMEM((HEAD, dec_len), f32),
            pltpu.SemaphoreType.DMA((heads,)),
            pltpu.SemaphoreType.DMA((heads,)),
            pltpu.SemaphoreType.DMA((heads,)),
            pltpu.SemaphoreType.DMA((heads,)),
            pltpu.SemaphoreType.DMA((2,)),
            pltpu.SemaphoreType.DMA((2, heads)),
        ],
        compiler_params=pltpu.CompilerParams(collective_id=0, has_side_effects=True, vmem_limit_bytes=60 * 2**20),
    )(pairs[0], queries[0], upstream[0])
    context, grad_query, grad_pairs = pl.pallas_call(
        place,
        out_shape=outs,
        in_specs=[hbm] * 3,
        out_specs=[hbm] * 3,
        scratch_shapes=[pltpu.VMEM(o.shape, o.dtype) for o in outs] + [pltpu.SemaphoreType.DMA((PARTS + 2,))] * 2,
        compiler_params=pltpu.CompilerParams(vmem_limit_bytes=20 * 2**20),
    )(*made)
    return (context[None], grad_query[None], grad_pairs[None])


def solution(mesh):
    rows = P("segment", ("seq", "tp"), None, None)
    columns = P("segment", None, ("seq", "tp"))
    return jax.shard_map(
        shards,
        mesh=mesh,
        in_specs=(rows, columns, columns),
        out_specs=(columns, columns, rows),
        check_vma=False,
    )
```

```python
import functools
import math

import jax
import jax.numpy as jnp
from jax import lax
from jax.experimental import pallas as pl
from jax.experimental.pallas import tpu as pltpu
from jax.sharding import PartitionSpec as P

MESH = pl.DeviceIdType.MESH
HEAD = 128
FACTOR = HEAD ** -0.5
LOG_SCALE = FACTOR * math.log2(math.e)
PIECES = 2
PARTS = 8
BATCH = 1
CHUNK = 512
UNROLL = 8
f32, bf16 = jnp.float32, jnp.bfloat16


def dot(a, b, ca, cb):
    return lax.dot_general(a, b, (((ca,), (cb,)), ((), ())), preferred_element_type=f32)


def split_rows():
    row = lax.broadcasted_iota(jnp.int32, (256, 256), 0)
    col = lax.broadcasted_iota(jnp.int32, (256, 256), 1)
    want = jnp.where(row < 128, 2 * row, 2 * row - 255)
    return (col == want).astype(bf16)


def spread(pos, sq, tp):
    j = lax.rem(5 * lax.rem(pos, 16) + 3, 16)
    dz, dx = j // 4, lax.rem(j, 4)
    z, x = lax.rem(sq // 4 + dz, 4), lax.rem(lax.rem(sq, 4) + dx, 4)
    return z * 4 + x, lax.rem(tp + dz + dx + pos // 16, 2)


def seen_from(pos):
    j = lax.rem(5 * lax.rem(pos, 16) + 3, 16)
    dz, dx = j // 4, lax.rem(j, 4)
    back = lax.rem(4 - dz, 4) * 4 + lax.rem(4 - dx, 4)
    return (pos // 16) * 16 + lax.rem((back + 13) * 13, 16)


def kernel(
    groups, segments, tps,
    pairs, q_hbm, g_hbm, ctx_hbm, dq_hbm, out,
    kv, q_v, g_v, ctx_v, dq_v, kk, vv, kt, vt, s_scr, p_scr, acc,
    kv_send, kv_recv, g_send, g_recv, in_sem, out_sem,
):
    seg, sq, tp = lax.axis_index("segment"), lax.axis_index("seq"), lax.axis_index("tp")
    me = sq * tps + tp
    nxt, prv = lax.rem(seg + 1, segments), lax.rem(seg + segments - 1, segments)
    rows = pairs.shape[0]
    enc_len, dec_len = kk.shape[0], q_v.shape[0]
    heads = kv.shape[0]
    width = heads * HEAD
    part = rows // PIECES

    barrier = pltpu.get_barrier_semaphore()

    def greet(i, c):
        pl.semaphore_signal(barrier, inc=1, device_id=(prv, i // tps, lax.rem(i, tps)), device_id_type=MESH)
        return c

    lax.fori_loop(0, groups, greet, 0)
    pl.semaphore_wait(barrier, groups)

    def kv_copy(h, pos, p):
        to_sq, to_tp = spread(pos, sq, tp)
        col = pl.multiple_of((to_sq * tps + to_tp) * width + h * HEAD, HEAD)
        piece = pl.ds(p * part, part)
        return pltpu.make_async_remote_copy(
            src_ref=pairs.at[piece, :, pl.ds(col, HEAD)], dst_ref=kv.at[h, seen_from(pos), piece],
            send_sem=kv_send.at[h], recv_sem=kv_recv.at[h],
            device_id=(nxt, to_sq, to_tp), device_id_type=MESH)

    def g_copy(h, pos, p):
        to_sq, to_tp = spread(pos, sq, tp)
        col = pl.multiple_of(me * width + h * HEAD, HEAD)
        piece = pl.ds(p * part, part)
        return pltpu.make_async_remote_copy(
            src_ref=kv.at[h, pos, piece], dst_ref=out.at[piece, :, pl.ds(col, HEAD)],
            send_sem=g_send.at[h], recv_sem=g_recv.at[h],
            device_id=(prv, to_sq, to_tp), device_id_type=MESH)

    for h in range(heads):
        def send(k, c):
            kv_copy(h, lax.rem(k, groups), k // groups).start()
            return c
        lax.fori_loop(0, groups * PIECES, send, 0)
    loads = [pltpu.make_async_copy(q_hbm, q_v, in_sem.at[0]), pltpu.make_async_copy(g_hbm, g_v, in_sem.at[1])]
    for load in loads:
        load.start()
    for load in loads:
        load.wait()

    sel = split_rows()
    sel_t = sel.T
    per = CHUNK // rows
    chunks = enc_len // CHUNK
    stores = []
    for h in range(heads):
        hs = slice(h * HEAD, (h + 1) * HEAD)
        flat = kv.at[h].reshape(groups, 2 * rows, HEAD)
        q, g = q_v.at[:, hs], g_v.at[:, hs]
        pltpu.make_async_copy(kv.at[h], kv.at[h], kv_recv.at[h]).wait()

        def split(i, c):
            for u in range(UNROLL):
                b = i * UNROLL + u
                y = dot(sel, flat[b], 1, 0).astype(bf16)
                r = pl.multiple_of(b * rows, rows)
                kk[pl.ds(r, rows), :] = y[:rows]
                vv[pl.ds(r, rows), :] = y[rows:]
                kt[:, pl.ds(r, rows)] = y[:rows].T
                vt[:, pl.ds(r, rows)] = y[rows:].T
            return c
        lax.fori_loop(0, groups // UNROLL, split, 0)

        def scores(i, m):
            o = pl.multiple_of(i * CHUNK, CHUNK)
            s = dot(kk[pl.ds(o, CHUNK), :], q[...], 1, 1)
            s_scr[pl.ds(o, CHUNK), :] = s
            return jnp.maximum(m, jnp.max(s.reshape(CHUNK // 8, 8, dec_len), axis=0))
        m = lax.fori_loop(0, chunks, scores, jnp.full((8, dec_len), -jnp.inf, f32))
        mc = jnp.max(m, axis=0, keepdims=True) * LOG_SCALE
        acc[...] = jnp.zeros_like(acc)

        def weigh(i, l):
            o = pl.multiple_of(i * CHUNK, CHUNK)
            p = jnp.exp2(s_scr[pl.ds(o, CHUNK), :] * LOG_SCALE - mc)
            pb = p.astype(bf16)
            p_scr[pl.ds(o, CHUNK), :] = pb
            acc[...] += dot(vt[:, pl.ds(o, CHUNK)], pb, 1, 0)
            return l + jnp.sum(p.reshape(CHUNK // 8, 8, dec_len), axis=0)
        l = lax.fori_loop(0, chunks, weigh, jnp.zeros((8, dec_len), f32))
        inv = 1.0 / jnp.sum(l, axis=0, keepdims=True)
        ctx = acc[...] * inv
        ctx_v[h] = ctx.T.astype(bf16)
        stores.append(pltpu.make_async_copy(ctx_v.at[h], ctx_hbm.at[:, hs], out_sem.at[0, h]))
        stores[-1].start()
        gf = g[...].astype(f32)
        row_dot = jnp.sum(gf.T * ctx, axis=0, keepdims=True)
        inv_col = jnp.broadcast_to(inv, (HEAD, dec_len)).T
        gn = (gf * inv_col).astype(bf16)
        qn = (q[...].astype(f32) * (inv_col * FACTOR)).astype(bf16)
        acc[...] = jnp.zeros_like(acc)

        def grads(i, c):
            o = pl.multiple_of(i * CHUNK, CHUNK)
            gw = dot(vv[pl.ds(o, CHUNK), :], g[...], 1, 1)
            pb = p_scr[pl.ds(o, CHUNK), :]
            ds = (pb.astype(f32) * (gw - row_dot)).astype(bf16)
            acc[...] += dot(kt[:, pl.ds(o, CHUNK)], ds, 1, 0)
            dk = dot(ds, qn, 1, 0).astype(bf16)
            dv = dot(pb, gn, 1, 0).astype(bf16)
            for u in range(per):
                a = u * rows
                x = jnp.concatenate([dk[a:a + rows], dv[a:a + rows]], axis=0)
                flat[i * per + u] = dot(sel_t, x, 1, 0).astype(bf16)

            @pl.when(lax.rem(i + 1, BATCH) == 0)
            def _():
                def send(k, c):
                    g_copy(h, (i + 1 - BATCH) * per + lax.rem(k, BATCH * per), k // (BATCH * per)).start()
                    return c
                lax.fori_loop(0, BATCH * per * PIECES, send, 0)
            return c
        lax.fori_loop(0, chunks, grads, 0)
        dq_v[h] = (acc[...] * (inv * FACTOR)).T.astype(bf16)
        stores.append(pltpu.make_async_copy(dq_v.at[h], dq_hbm.at[:, hs], out_sem.at[1, h]))
        stores[-1].start()

    for store in stores:
        store.wait()
    for h in range(heads):
        for sem in (kv_send, g_send, g_recv):
            pltpu.make_async_copy(kv.at[h], kv.at[h], sem.at[h]).wait()


def place(ctx, dq, grads, ctx_out, dq_out, grads_out, sem):
    copies = [
        pltpu.make_async_copy(src, dst, sem.at[i])
        for i, (src, dst) in enumerate(((grads, grads_out), (ctx, ctx_out), (dq, dq_out)))
    ]
    for copy in copies:
        copy.start()
    for copy in copies:
        copy.wait()


def shards(pairs, queries, upstream):
    groups = lax.axis_size("seq") * lax.axis_size("tp")
    _, rows, _, columns = pairs.shape
    _, dec_len, width = queries.shape
    heads = width // HEAD
    enc_len = rows * groups
    hbm = pl.BlockSpec(memory_space=pl.ANY)
    outs = [
        jax.ShapeDtypeStruct((dec_len, width), bf16),
        jax.ShapeDtypeStruct((dec_len, width), bf16),
        jax.ShapeDtypeStruct((rows, 2, columns), bf16),
    ]
    made = pl.pallas_call(
        functools.partial(kernel, groups, lax.axis_size("segment"), lax.axis_size("tp")),
        out_shape=[pltpu.VMEM(o.shape, o.dtype) for o in outs],
        in_specs=[hbm] * 3,
        out_specs=[hbm] * 3,
        scratch_shapes=[
            pltpu.VMEM((heads, groups, rows, 2, HEAD), bf16),
            pltpu.VMEM((dec_len, width), bf16),
            pltpu.VMEM((dec_len, width), bf16),
            pltpu.VMEM((heads, dec_len, HEAD), bf16),
            pltpu.VMEM((heads, dec_len, HEAD), bf16),
            pltpu.VMEM((enc_len, HEAD), bf16),
            pltpu.VMEM((enc_len, HEAD), bf16),
            pltpu.VMEM((HEAD, enc_len), bf16),
            pltpu.VMEM((HEAD, enc_len), bf16),
            pltpu.VMEM((enc_len, dec_len), f32),
            pltpu.VMEM((enc_len, dec_len), bf16),
            pltpu.VMEM((HEAD, dec_len), f32),
            pltpu.SemaphoreType.DMA((heads,)),
            pltpu.SemaphoreType.DMA((heads,)),
            pltpu.SemaphoreType.DMA((heads,)),
            pltpu.SemaphoreType.DMA((heads,)),
            pltpu.SemaphoreType.DMA((2,)),
            pltpu.SemaphoreType.DMA((2, heads)),
        ],
        compiler_params=pltpu.CompilerParams(collective_id=0, has_side_effects=True, vmem_limit_bytes=54 * 2**20),
    )(pairs[0], queries[0], upstream[0])
    context, grad_query, grad_pairs = pl.pallas_call(
        place,
        out_shape=outs,
        in_specs=[pl.BlockSpec(memory_space=pltpu.VMEM)] * 3,
        out_specs=[hbm] * 3,
        scratch_shapes=[pltpu.SemaphoreType.DMA((3,))],
        compiler_params=pltpu.CompilerParams(vmem_limit_bytes=20 * 2**20),
    )(*made)
    return (context[None], grad_query[None], grad_pairs[None])


def solution(mesh):
    rows = P("segment", ("seq", "tp"), None, None)
    columns = P("segment", None, ("seq", "tp"))
    return jax.shard_map(
        shards,
        mesh=mesh,
        in_specs=(rows, columns, columns),
        out_specs=(columns, columns, rows),
        check_vma=False,
    )
```

```python
import functools
import math

import jax
import jax.numpy as jnp
from jax import lax
from jax.experimental import pallas as pl
from jax.experimental.pallas import tpu as pltpu
from jax.sharding import PartitionSpec as P

MESH = pl.DeviceIdType.MESH
HEAD = 128
FACTOR = HEAD ** -0.5
LOG_SCALE = FACTOR * math.log2(math.e)
PIECES = 2
HALF = 16
CHUNK = 512
f32, bf16 = jnp.float32, jnp.bfloat16


def dot(a, b, ca, cb):
    return lax.dot_general(a, b, (((ca,), (cb,)), ((), ())), preferred_element_type=f32)


def split_rows():
    row = lax.broadcasted_iota(jnp.int32, (256, 256), 0)
    col = lax.broadcasted_iota(jnp.int32, (256, 256), 1)
    want = jnp.where(row < 128, 2 * row, 2 * row - 255)
    return (col == want).astype(bf16)


def spread(pos, sq, tp):
    j = lax.rem(5 * lax.rem(pos, 16) + 3, 16)
    dz, dx = j // 4, lax.rem(j, 4)
    z, x = lax.rem(sq // 4 + dz, 4), lax.rem(lax.rem(sq, 4) + dx, 4)
    return z * 4 + x, lax.rem(tp + dz + dx + pos // 16, 2)


def seen_from(pos):
    j = lax.rem(5 * lax.rem(pos, 16) + 3, 16)
    dz, dx = j // 4, lax.rem(j, 4)
    back = lax.rem(4 - dz, 4) * 4 + lax.rem(4 - dx, 4)
    return (pos // 16) * 16 + lax.rem((back + 13) * 13, 16)


def kernel(
    groups, segments, tps,
    pairs, q_hbm, g_hbm, ctx_hbm, dq_hbm, out,
    kv, q_v, g_v, ctx_v, dq_v, vv, kt, vt, s_scr, p_scr, acc,
    kv_send, kv_recv, g_send, g_recv, in_sem, out_sem,
):
    seg, sq, tp = lax.axis_index("segment"), lax.axis_index("seq"), lax.axis_index("tp")
    me = sq * tps + tp
    nxt, prv = lax.rem(seg + 1, segments), lax.rem(seg + segments - 1, segments)
    rows = pairs.shape[0]
    enc_len, dec_len = vv.shape[0], q_v.shape[0]
    heads = kv.shape[0]
    width = heads * HEAD
    part = rows // PIECES

    barrier = pltpu.get_barrier_semaphore()

    def greet(i, c):
        pl.semaphore_signal(barrier, inc=1, device_id=(prv, i // tps, lax.rem(i, tps)), device_id_type=MESH)
        return c

    lax.fori_loop(0, groups, greet, 0)
    pl.semaphore_wait(barrier, groups)

    def kv_copy(h, pos, p):
        to_sq, to_tp = spread(pos, sq, tp)
        col = pl.multiple_of((to_sq * tps + to_tp) * width + h * HEAD, HEAD)
        piece = pl.ds(p * part, part)
        return pltpu.make_async_remote_copy(
            src_ref=pairs.at[piece, :, pl.ds(col, HEAD)], dst_ref=kv.at[h, seen_from(pos), piece],
            send_sem=kv_send.at[h], recv_sem=kv_recv.at[h, pos // HALF],
            device_id=(nxt, to_sq, to_tp), device_id_type=MESH)

    def g_copies(h, pos):
        to_sq, to_tp = spread(pos, sq, tp)
        col = pl.multiple_of(me * width + h * HEAD, HEAD)
        pieces = [pl.ds(p * part, part) for p in range(PIECES)]
        return [pltpu.make_async_remote_copy(
            src_ref=kv.at[h, pos, piece], dst_ref=out.at[piece, :, pl.ds(col, HEAD)],
            send_sem=g_send.at[h], recv_sem=g_recv.at[h],
            device_id=(prv, to_sq, to_tp), device_id_type=MESH) for piece in pieces]

    for h in range(heads):
        def send(k, c):
            half, inner = k // (HALF * PIECES), lax.rem(k, HALF * PIECES)
            kv_copy(h, half * HALF + lax.rem(inner, HALF), inner // HALF).start()
            return c
        lax.fori_loop(0, groups * PIECES, send, 0)
    loads = [pltpu.make_async_copy(q_hbm, q_v, in_sem.at[0]), pltpu.make_async_copy(g_hbm, g_v, in_sem.at[1])]
    for load in loads:
        load.start()
    for load in loads:
        load.wait()

    vt[HEAD:, :] = jnp.ones((16, enc_len), bf16)
    sel = split_rows()
    sel_t = sel.T
    per = CHUNK // rows
    chunks = enc_len // CHUNK
    stores = []
    for h in range(heads):
        hs = slice(h * HEAD, (h + 1) * HEAD)
        flat = kv.at[h].reshape(groups, 2 * rows, HEAD)
        q, g = q_v.at[:, hs], g_v.at[:, hs]

        def scores(i, m):
            o = pl.multiple_of(i * CHUNK, CHUNK)
            keys = []
            for u in range(per):
                y = dot(sel, flat[i * per + u], 1, 0).astype(bf16)
                r = pl.multiple_of(o + u * rows, rows)
                keys.append(y[:rows])
                vv[pl.ds(r, rows), :] = y[rows:]
                kt[:, pl.ds(r, rows)] = y[:rows].T
                vt[:HEAD, pl.ds(r, rows)] = y[rows:].T
            s = dot(jnp.concatenate(keys, axis=0), q[...], 1, 1)
            s_scr[pl.ds(o, CHUNK), :] = s
            return jnp.maximum(m, jnp.max(s.reshape(CHUNK // 8, 8, dec_len), axis=0))
        m = jnp.full((8, dec_len), -jnp.inf, f32)
        for half in range(groups // HALF):
            arrived = kv.at[h, pl.ds(half * HALF, HALF)]
            pltpu.make_async_copy(arrived, arrived, kv_recv.at[h, half]).wait()
            m = lax.fori_loop(half * HALF // per, (half + 1) * HALF // per, scores, m)
        mc = jnp.max(m, axis=0, keepdims=True) * LOG_SCALE
        acc[...] = jnp.zeros_like(acc)

        def weigh(i, c):
            o = pl.multiple_of(i * CHUNK, CHUNK)
            pb = jnp.exp2(s_scr[pl.ds(o, CHUNK), :] * LOG_SCALE - mc).astype(bf16)
            p_scr[pl.ds(o, CHUNK), :] = pb
            acc[...] += dot(vt[:, pl.ds(o, CHUNK)], pb, 1, 0)
            return c
        lax.fori_loop(0, chunks, weigh, 0)
        inv = 1.0 / acc[HEAD:HEAD + 1, :]
        ctx = acc[:HEAD, :] * inv
        ctx_v[h] = ctx.T.astype(bf16)
        stores.append(pltpu.make_async_copy(ctx_v.at[h], ctx_hbm.at[:, hs], out_sem.at[0, h]))
        stores[-1].start()
        gf = g[...].astype(f32)
        row_dot = jnp.sum(gf.T * ctx, axis=0, keepdims=True)
        inv_col = jnp.broadcast_to(inv, (HEAD, dec_len)).T
        gn = (gf * inv_col).astype(bf16)
        qn = (q[...].astype(f32) * (inv_col * FACTOR)).astype(bf16)
        acc[:HEAD, :] = jnp.zeros((HEAD, dec_len), f32)

        def grads(i, c):
            o = pl.multiple_of(i * CHUNK, CHUNK)
            gw = dot(vv[pl.ds(o, CHUNK), :], g[...], 1, 1)
            pb = p_scr[pl.ds(o, CHUNK), :]
            ds = (pb.astype(f32) * (gw - row_dot)).astype(bf16)
            acc[:HEAD, :] += dot(kt[:, pl.ds(o, CHUNK)], ds, 1, 0)
            dk = dot(ds, qn, 1, 0).astype(bf16)
            dv = dot(pb, gn, 1, 0).astype(bf16)
            for u in range(per):
                a = u * rows
                x = jnp.concatenate([dk[a:a + rows], dv[a:a + rows]], axis=0)
                flat[i * per + u] = dot(sel_t, x, 1, 0).astype(bf16)

            for u in range(per):
                for copy in g_copies(h, i * per + u):
                    copy.start()
            return c
        lax.fori_loop(0, chunks, grads, 0)
        dq_v[h] = (acc[:HEAD, :] * (inv * FACTOR)).T.astype(bf16)
        stores.append(pltpu.make_async_copy(dq_v.at[h], dq_hbm.at[:, hs], out_sem.at[1, h]))
        stores[-1].start()

    for store in stores:
        store.wait()
    for h in range(heads):
        for sem in (kv_send, g_send, g_recv):
            pltpu.make_async_copy(kv.at[h], kv.at[h], sem.at[h]).wait()


def place(ctx, dq, grads, ctx_out, dq_out, grads_out, sem):
    copies = [
        pltpu.make_async_copy(src, dst, sem.at[i])
        for i, (src, dst) in enumerate(((grads, grads_out), (ctx, ctx_out), (dq, dq_out)))
    ]
    for copy in copies:
        copy.start()
    for copy in copies:
        copy.wait()


def shards(pairs, queries, upstream):
    groups = lax.axis_size("seq") * lax.axis_size("tp")
    _, rows, _, columns = pairs.shape
    _, dec_len, width = queries.shape
    heads = width // HEAD
    enc_len = rows * groups
    hbm = pl.BlockSpec(memory_space=pl.ANY)
    outs = [
        jax.ShapeDtypeStruct((dec_len, width), bf16),
        jax.ShapeDtypeStruct((dec_len, width), bf16),
        jax.ShapeDtypeStruct((rows, 2, columns), bf16),
    ]
    made = pl.pallas_call(
        functools.partial(kernel, groups, lax.axis_size("segment"), lax.axis_size("tp")),
        out_shape=[pltpu.VMEM(o.shape, o.dtype) for o in outs],
        in_specs=[hbm] * 3,
        out_specs=[hbm] * 3,
        scratch_shapes=[
            pltpu.VMEM((heads, groups, rows, 2, HEAD), bf16),
            pltpu.VMEM((dec_len, width), bf16),
            pltpu.VMEM((dec_len, width), bf16),
            pltpu.VMEM((heads, dec_len, HEAD), bf16),
            pltpu.VMEM((heads, dec_len, HEAD), bf16),
            pltpu.VMEM((enc_len, HEAD), bf16),
            pltpu.VMEM((HEAD, enc_len), bf16),
            pltpu.VMEM((HEAD + 16, enc_len), bf16),
            pltpu.VMEM((enc_len, dec_len), f32),
            pltpu.VMEM((enc_len, dec_len), bf16),
            pltpu.VMEM((HEAD + 16, dec_len), f32),
            pltpu.SemaphoreType.DMA((heads,)),
            pltpu.SemaphoreType.DMA((heads, groups // HALF)),
            pltpu.SemaphoreType.DMA((heads,)),
            pltpu.SemaphoreType.DMA((heads,)),
            pltpu.SemaphoreType.DMA((2,)),
            pltpu.SemaphoreType.DMA((2, heads)),
        ],
        compiler_params=pltpu.CompilerParams(collective_id=0, has_side_effects=True, vmem_limit_bytes=54 * 2**20),
    )(pairs[0], queries[0], upstream[0])
    context, grad_query, grad_pairs = pl.pallas_call(
        place,
        out_shape=outs,
        in_specs=[pl.BlockSpec(memory_space=pltpu.VMEM)] * 3,
        out_specs=[hbm] * 3,
        scratch_shapes=[pltpu.SemaphoreType.DMA((3,))],
        compiler_params=pltpu.CompilerParams(vmem_limit_bytes=20 * 2**20),
    )(*made)
    return (context[None], grad_query[None], grad_pairs[None])


def solution(mesh):
    rows = P("segment", ("seq", "tp"), None, None)
    columns = P("segment", None, ("seq", "tp"))
    return jax.shard_map(
        shards,
        mesh=mesh,
        in_specs=(rows, columns, columns),
        out_specs=(columns, columns, rows),
        check_vma=False,
    )
```

```python
import functools
import math

import jax
import jax.numpy as jnp
from jax import lax
from jax.experimental import pallas as pl
from jax.experimental.pallas import tpu as pltpu
from jax.sharding import PartitionSpec as P

MESH = pl.DeviceIdType.MESH
HEAD = 128
FACTOR = HEAD ** -0.5
LOG_SCALE = FACTOR * math.log2(math.e)
PIECES = 2
IN_PIECES = 4
HALF = 32
CHUNK = 512
f32, bf16 = jnp.float32, jnp.bfloat16


def dot(a, b, ca, cb):
    return lax.dot_general(a, b, (((ca,), (cb,)), ((), ())), preferred_element_type=f32)


def split_rows():
    row = lax.broadcasted_iota(jnp.int32, (256, 256), 0)
    col = lax.broadcasted_iota(jnp.int32, (256, 256), 1)
    want = jnp.where(row < 128, 2 * row, 2 * row - 255)
    return (col == want).astype(bf16)


def spread(pos, sq, tp):
    j = lax.rem(5 * lax.rem(pos, 16) + 3, 16)
    dz, dx = j // 4, lax.rem(j, 4)
    z, x = lax.rem(sq // 4 + dz, 4), lax.rem(lax.rem(sq, 4) + dx, 4)
    return z * 4 + x, lax.rem(tp + dz + dx + pos // 16, 2)


def seen_from(pos):
    j = lax.rem(5 * lax.rem(pos, 16) + 3, 16)
    dz, dx = j // 4, lax.rem(j, 4)
    back = lax.rem(4 - dz, 4) * 4 + lax.rem(4 - dx, 4)
    return (pos // 16) * 16 + lax.rem((back + 13) * 13, 16)


def kernel(
    groups, segments, tps,
    pairs, q_hbm, g_hbm, ctx_hbm, dq_hbm, out,
    kv, q_v, g_v, ctx_v, dq_v, vv, kt, vt, s_scr, p_scr, acc,
    kv_send, kv_recv, g_send, g_recv, in_sem, out_sem,
):
    seg, sq, tp = lax.axis_index("segment"), lax.axis_index("seq"), lax.axis_index("tp")
    me = sq * tps + tp
    nxt, prv = lax.rem(seg + 1, segments), lax.rem(seg + segments - 1, segments)
    rows = pairs.shape[0]
    enc_len, dec_len = vv.shape[0], q_v.shape[0]
    heads = kv.shape[0]
    width = heads * HEAD
    part = rows // PIECES
    in_part = rows // IN_PIECES

    barrier = pltpu.get_barrier_semaphore()

    def greet(i, c):
        pl.semaphore_signal(barrier, inc=1, device_id=(prv, i // tps, lax.rem(i, tps)), device_id_type=MESH)
        return c

    lax.fori_loop(0, groups, greet, 0)
    pl.semaphore_wait(barrier, groups)

    def kv_copy(h, pos, p):
        to_sq, to_tp = spread(pos, sq, tp)
        col = pl.multiple_of((to_sq * tps + to_tp) * width + h * HEAD, HEAD)
        piece = pl.ds(p * in_part, in_part)
        return pltpu.make_async_remote_copy(
            src_ref=pairs.at[piece, :, pl.ds(col, HEAD)], dst_ref=kv.at[h, seen_from(pos), piece],
            send_sem=kv_send.at[h], recv_sem=kv_recv.at[h, pos // HALF],
            device_id=(nxt, to_sq, to_tp), device_id_type=MESH)

    def g_copies(h, pos):
        to_sq, to_tp = spread(pos, sq, tp)
        col = pl.multiple_of(me * width + h * HEAD, HEAD)
        pieces = [pl.ds(p * part, part) for p in range(PIECES)]
        return [pltpu.make_async_remote_copy(
            src_ref=kv.at[h, pos, piece], dst_ref=out.at[piece, :, pl.ds(col, HEAD)],
            send_sem=g_send.at[h], recv_sem=g_recv.at[h],
            device_id=(prv, to_sq, to_tp), device_id_type=MESH) for piece in pieces]

    for h in range(heads):
        def send(k, c):
            half, inner = k // (HALF * IN_PIECES), lax.rem(k, HALF * IN_PIECES)
            kv_copy(h, half * HALF + lax.rem(inner, HALF), inner // HALF).start()
            return c
        lax.fori_loop(0, groups * IN_PIECES, send, 0)
    loads = [pltpu.make_async_copy(q_hbm, q_v, in_sem.at[0]), pltpu.make_async_copy(g_hbm, g_v, in_sem.at[1])]
    for load in loads:
        load.start()
    for load in loads:
        load.wait()

    vt[HEAD:, :] = jnp.ones((16, enc_len), bf16)
    sel = split_rows()
    sel_t = sel.T
    per = CHUNK // rows
    chunks = enc_len // CHUNK
    stores = []
    for h in range(heads):
        hs = slice(h * HEAD, (h + 1) * HEAD)
        flat = kv.at[h].reshape(groups, 2 * rows, HEAD)
        q, g = q_v.at[:, hs], g_v.at[:, hs]

        def scores(i, m):
            o = pl.multiple_of(i * CHUNK, CHUNK)
            keys = []
            for u in range(per):
                y = dot(sel, flat[i * per + u], 1, 0).astype(bf16)
                r = pl.multiple_of(o + u * rows, rows)
                keys.append(y[:rows])
                vv[pl.ds(r, rows), :] = y[rows:]
                kt[:, pl.ds(r, rows)] = y[:rows].T
                vt[:HEAD, pl.ds(r, rows)] = y[rows:].T
            s = dot(jnp.concatenate(keys, axis=0), q[...], 1, 1)
            s_scr[pl.ds(o, CHUNK), :] = s
            return jnp.maximum(m, jnp.max(s.reshape(CHUNK // 8, 8, dec_len), axis=0))
        m = jnp.full((8, dec_len), -jnp.inf, f32)
        for half in range(groups // HALF):
            arrived = kv.at[h, pl.ds(half * HALF, HALF)]
            pltpu.make_async_copy(arrived, arrived, kv_recv.at[h, half]).wait()
            m = lax.fori_loop(half * HALF // per, (half + 1) * HALF // per, scores, m)
        mc = jnp.max(m, axis=0, keepdims=True) * LOG_SCALE
        acc[...] = jnp.zeros_like(acc)

        def weigh(i, c):
            o = pl.multiple_of(i * CHUNK, CHUNK)
            pb = jnp.exp2(s_scr[pl.ds(o, CHUNK), :] * LOG_SCALE - mc).astype(bf16)
            p_scr[pl.ds(o, CHUNK), :] = pb
            acc[...] += dot(vt[:, pl.ds(o, CHUNK)], pb, 1, 0)
            return c
        lax.fori_loop(0, chunks, weigh, 0)
        inv = 1.0 / acc[HEAD:HEAD + 1, :]
        ctx = acc[:HEAD, :] * inv
        ctx_v[h] = ctx.T.astype(bf16)
        stores.append(pltpu.make_async_copy(ctx_v.at[h], ctx_hbm.at[:, hs], out_sem.at[0, h]))
        stores[-1].start()
        gf = g[...].astype(f32)
        row_dot = jnp.sum(gf.T * ctx, axis=0, keepdims=True)
        inv_col = jnp.broadcast_to(inv, (HEAD, dec_len)).T
        gn = (gf * inv_col).astype(bf16)
        qn = (q[...].astype(f32) * (inv_col * FACTOR)).astype(bf16)
        acc[:HEAD, :] = jnp.zeros((HEAD, dec_len), f32)

        def grads(i, c):
            o = pl.multiple_of(i * CHUNK, CHUNK)
            gw = dot(vv[pl.ds(o, CHUNK), :], g[...], 1, 1)
            pb = p_scr[pl.ds(o, CHUNK), :]
            ds = (pb.astype(f32) * (gw - row_dot)).astype(bf16)
            acc[:HEAD, :] += dot(kt[:, pl.ds(o, CHUNK)], ds, 1, 0)
            dk = dot(ds, qn, 1, 0).astype(bf16)
            dv = dot(pb, gn, 1, 0).astype(bf16)
            for u in range(per):
                a = u * rows
                x = jnp.concatenate([dk[a:a + rows], dv[a:a + rows]], axis=0)
                flat[i * per + u] = dot(sel_t, x, 1, 0).astype(bf16)

            for u in range(per):
                for copy in g_copies(h, i * per + u):
                    copy.start()
            return c
        lax.fori_loop(0, chunks, grads, 0)
        dq_v[h] = (acc[:HEAD, :] * (inv * FACTOR)).T.astype(bf16)
        stores.append(pltpu.make_async_copy(dq_v.at[h], dq_hbm.at[:, hs], out_sem.at[1, h]))
        stores[-1].start()

    for store in stores:
        store.wait()
    for h in range(heads):
        for sem in (kv_send, g_send, g_recv):
            pltpu.make_async_copy(kv.at[h], kv.at[h], sem.at[h]).wait()


def place(ctx, dq, grads, ctx_out, dq_out, grads_out, sem):
    copies = [
        pltpu.make_async_copy(src, dst, sem.at[i])
        for i, (src, dst) in enumerate(((grads, grads_out), (ctx, ctx_out), (dq, dq_out)))
    ]
    for copy in copies:
        copy.start()
    for copy in copies:
        copy.wait()


def shards(pairs, queries, upstream):
    groups = lax.axis_size("seq") * lax.axis_size("tp")
    _, rows, _, columns = pairs.shape
    _, dec_len, width = queries.shape
    heads = width // HEAD
    enc_len = rows * groups
    hbm = pl.BlockSpec(memory_space=pl.ANY)
    outs = [
        jax.ShapeDtypeStruct((dec_len, width), bf16),
        jax.ShapeDtypeStruct((dec_len, width), bf16),
        jax.ShapeDtypeStruct((rows, 2, columns), bf16),
    ]
    made = pl.pallas_call(
        functools.partial(kernel, groups, lax.axis_size("segment"), lax.axis_size("tp")),
        out_shape=[pltpu.VMEM(o.shape, o.dtype) for o in outs],
        in_specs=[hbm] * 3,
        out_specs=[hbm] * 3,
        scratch_shapes=[
            pltpu.VMEM((heads, groups, rows, 2, HEAD), bf16),
            pltpu.VMEM((dec_len, width), bf16),
            pltpu.VMEM((dec_len, width), bf16),
            pltpu.VMEM((heads, dec_len, HEAD), bf16),
            pltpu.VMEM((heads, dec_len, HEAD), bf16),
            pltpu.VMEM((enc_len, HEAD), bf16),
            pltpu.VMEM((HEAD, enc_len), bf16),
            pltpu.VMEM((HEAD + 16, enc_len), bf16),
            pltpu.VMEM((enc_len, dec_len), f32),
            pltpu.VMEM((enc_len, dec_len), bf16),
            pltpu.VMEM((HEAD + 16, dec_len), f32),
            pltpu.SemaphoreType.DMA((heads,)),
            pltpu.SemaphoreType.DMA((heads, groups // HALF)),
            pltpu.SemaphoreType.DMA((heads,)),
            pltpu.SemaphoreType.DMA((heads,)),
            pltpu.SemaphoreType.DMA((2,)),
            pltpu.SemaphoreType.DMA((2, heads)),
        ],
        compiler_params=pltpu.CompilerParams(collective_id=0, has_side_effects=True, vmem_limit_bytes=54 * 2**20),
    )(pairs[0], queries[0], upstream[0])
    context, grad_query, grad_pairs = pl.pallas_call(
        place,
        out_shape=outs,
        in_specs=[pl.BlockSpec(memory_space=pltpu.VMEM)] * 3,
        out_specs=[hbm] * 3,
        scratch_shapes=[pltpu.SemaphoreType.DMA((3,))],
        compiler_params=pltpu.CompilerParams(vmem_limit_bytes=20 * 2**20),
    )(*made)
    return (context[None], grad_query[None], grad_pairs[None])


def solution(mesh):
    rows = P("segment", ("seq", "tp"), None, None)
    columns = P("segment", None, ("seq", "tp"))
    return jax.shard_map(
        shards,
        mesh=mesh,
        in_specs=(rows, columns, columns),
        out_specs=(columns, columns, rows),
        check_vma=False,
    )
```
